32 devices in a mesh: blk: 16 (over z, x, core), uly: 2 (over y).
Axes of the slice: x: 2, y: 2, z: 4, core: 2. Of those that a mesh axis runs over, the one named last changes fastest.
Arguments:
- queries: bfloat16 [16384, 2048], P(('blk', 'uly'))
- keys: bfloat16 [16384, 256], P(('blk', 'uly'))
- values: bfloat16 [16384, 256], P(('blk', 'uly')), may hold values from -6 to 6
- chosen: int32 [32, 2, 2], replicated, may hold values from 0 to 30, as said below
Outputs:
- attended: bfloat16 [16384, 2048], P(('blk', 'uly'))
The draws below stay inside these ranges and needn't reach their ends.
Inputs may be any that keep to these rules, and one draw needn't show every extreme that they name: For attention block j and key-value head h, chosen[j, h, 0] and chosen[j, h, 1] differ; for j >= 2 both are below j; for j < 2 at least one is not below j. An id that is not below j selects nothing.
All inputs are finite; a program needn't handle non-finite values.
Results may differ from the reference program's by a relative error of at most 0.0046.
Values may be sent and summed in bfloat16 or wider, within the bound.
No kernel may reach another device: no remote copies, remote signals or barrier semaphores. Data moves between devices by JAX's collectives and lax.ppermute only.
A program may use at most 64 MiB of HBM per device.

```python
import jax
import jax.numpy as jnp
from jax import lax

BS = 512
HD = 128
GROUP = 8
KVH = 2
TOKENS = 16384
NBLOCKS = 32


def draw_queries(key, part):
    shape = (TOKENS, KVH, GROUP, HD)
    own_key = jax.random.fold_in(key, 1)
    base = jnp.clip(jax.random.normal(own_key, shape, jnp.float32), -6.0, 6.0)
    return base.reshape(TOKENS, KVH * GROUP * HD).astype(jnp.bfloat16)


def draw_keys(key, part):
    shape = (TOKENS, KVH, HD)
    own_key = jax.random.fold_in(key, 2)
    base = jnp.clip(jax.random.normal(own_key, shape, jnp.float32), -6.0, 6.0)
    return base.reshape(TOKENS, KVH * HD).astype(jnp.bfloat16)


def draw_chosen(key, part):
    block = jnp.arange(NBLOCKS, dtype=jnp.int32)[:, None]
    heads = jnp.arange(KVH, dtype=jnp.int32)[None, :]
    first = jax.random.randint(jax.random.fold_in(key, 5), (NBLOCKS, KVH), 0, jnp.maximum(block, 1))
    first = jnp.where((block == NBLOCKS - 1) & (heads == 0), NBLOCKS - 2, first).astype(jnp.int32)
    other = jax.random.randint(jax.random.fold_in(key, 6), (NBLOCKS, KVH), 0, jnp.maximum(block - 1, 1))
    second = other + (other >= first).astype(jnp.int32)
    return jnp.stack([first, second], axis=-1).astype(jnp.int32)


def steps_of(rng, shape, cuts, low, largest):
    def one(dim, parts):
        draws = jax.random.uniform(jax.random.fold_in(jax.random.fold_in(rng, 6), dim), (parts,), jnp.float32, low / len(cuts), largest / len(cuts))
        return jnp.repeat(jnp.exp(draws), shape[dim] // parts).reshape((-1,) + (1,) * (len(shape) - dim - 1))

    loudness = one(*cuts[0])
    for cut in cuts[1:]:
        loudness = loudness * one(*cut)
    return loudness


def gaussian(key, extent, deviation, reach, shards=(), kind=jnp.bfloat16):
    loudness = steps_of(key, extent, shards, -0.22, 0.18) if shards else 1.0
    drawn = jax.random.normal(key, extent, jnp.float32) * deviation * loudness
    return jnp.minimum(jnp.maximum(drawn, -reach), reach).astype(kind)


def setup_inputs(seed: int = 0) -> dict:
    splits = jax.random.split(jax.random.key(seed), 5)
    queries = draw_queries(jax.random.fold_in(splits[4], 71), 0)
    keys = draw_keys(jax.random.fold_in(splits[4], 71), 0)
    values = gaussian(splits[2], (TOKENS, KVH * HD), 1.0, 6.0, ((0, 32),))
    chosen = draw_chosen(jax.random.fold_in(splits[4], 71), 0)
    return dict(queries=queries, keys=keys, values=values, chosen=chosen)


def reference(queries, keys, values, chosen):
    scale = HD ** -0.5
    q_blocks = queries.reshape(NBLOCKS, BS, KVH, GROUP, HD)
    key_table = jnp.transpose(keys.reshape(NBLOCKS, BS, KVH, HD), (2, 0, 1, 3))
    value_table = jnp.transpose(values.reshape(NBLOCKS, BS, KVH, HD), (2, 0, 1, 3))
    causal = jnp.arange(BS, dtype=jnp.int32)[None, :] <= jnp.arange(BS, dtype=jnp.int32)[:, None]
    head_rows = jnp.arange(KVH, dtype=jnp.int32)[:, None]

    def one_block(block):
        query_rows = q_blocks[block].astype(jnp.float32)
        picks = chosen[block]
        key_rows = jnp.concatenate([key_table[:, block][:, None], key_table[head_rows, picks]], axis=1)
        value_rows = jnp.concatenate([value_table[:, block][:, None], value_table[head_rows, picks]], axis=1)
        key_rows = key_rows.reshape(KVH, 3 * BS, HD).astype(jnp.float32)
        value_rows = value_rows.reshape(KVH, 3 * BS, HD).astype(jnp.float32)
        scores = jnp.einsum("tkgd,ksd->kgts", query_rows, key_rows) * scale
        usable = picks < block
        routed = jnp.broadcast_to(usable[:, None, :, None], (KVH, BS, 2, BS)).reshape(KVH, BS, 2 * BS)
        own = jnp.broadcast_to(causal[None], (KVH, BS, BS))
        allowed = jnp.concatenate([own, routed], axis=2)[:, None]
        scores = jnp.where(allowed, scores, -jnp.inf)
        top = jnp.max(scores, axis=-1, keepdims=True)
        weights = jnp.exp(scores - top)
        total = jnp.sum(weights, axis=-1, keepdims=True)
        rounded = lax.optimization_barrier(weights.astype(jnp.bfloat16)).astype(jnp.float32)
        summed = jnp.einsum("kgts,ksd->tkgd", rounded, value_rows)
        return (summed / jnp.transpose(total, (2, 0, 1, 3))).astype(jnp.bfloat16)

    outputs = lax.map(one_block, jnp.arange(NBLOCKS, dtype=jnp.int32))
    return outputs.reshape(TOKENS, KVH * GROUP * HD)
```

```python
import functools
import math

import jax
import jax.numpy as jnp
from jax import lax
from jax.experimental import pallas as pl
from jax.experimental.pallas import tpu as pltpu
from jax.sharding import PartitionSpec as P

BS = 512
HD = 128
GROUP = 8
AXES = ("blk", "uly")
TILE = 256
HEADS_A_STEP = 4
EXPONENT = HD ** (-0.5) * math.log2(math.e)


def scores_of(rows, key_rows):
    return lax.dot_general(
        rows, key_rows, (((1,), (1,)), ((), ())), preferred_element_type=jnp.float32
    )


def lane_max(scores):
    parts = [scores[:, i : i + HD] for i in range(0, scores.shape[1], HD)]
    return functools.reduce(jnp.maximum, parts)


def attend_kernel(usable, q_ref, k_ref, v_ref, routed_ref, out_ref):
    head = pl.program_id(0) * HEADS_A_STEP // GROUP
    use = [usable[head, s] != 0 for s in range(2)]
    ones = jnp.ones((BS, HD), jnp.bfloat16)
    own_k = k_ref[...]
    own_v = jnp.concatenate([v_ref[...], ones], axis=1)
    routed_k = [routed_ref[:, s, :, :HD].reshape(BS, HD) for s in range(2)]
    routed_v = [
        jnp.concatenate([routed_ref[:, s, :, HD:].reshape(BS, HD), ones], axis=1) for s in range(2)
    ]
    causal = lax.broadcasted_iota(jnp.int32, (TILE, TILE), 1) <= lax.broadcasted_iota(
        jnp.int32, (TILE, TILE), 0
    )

    def first(item):
        col, start = item
        rows = q_ref[start : start + TILE, col : col + HD]
        return scores_of(rows, own_k[: start + TILE]), [scores_of(rows, k) for k in routed_k]

    def second(item, scored):
        col, start = item
        own, routed = scored
        diagonal = jnp.where(causal, own[:, start:], -jnp.inf)
        own = jnp.concatenate([own[:, :start], diagonal], axis=1) if start else diagonal
        top = lane_max(own)
        for s in range(2):
            top = jnp.maximum(top, jnp.where(use[s], lane_max(routed[s]), -jnp.inf))
        top = jnp.max(top, axis=1, keepdims=True) * EXPONENT
        weights = jnp.exp2(own * EXPONENT - top).astype(jnp.bfloat16)
        both = jnp.dot(weights, own_v[: start + TILE], preferred_element_type=jnp.float32)
        for s in range(2):
            bound = jnp.where(use[s], top, jnp.inf)
            weights = jnp.exp2(routed[s] * EXPONENT - bound).astype(jnp.bfloat16)
            both = both + jnp.dot(weights, routed_v[s], preferred_element_type=jnp.float32)
        out_ref[start : start + TILE, col : col + HD] = (both[:, :HD] / both[:, HD:]).astype(
            out_ref.dtype
        )

    items = [(h * HD, t) for h in range(HEADS_A_STEP) for t in range(0, BS, TILE)]
    held = first(items[0])
    for item, following in zip(items, items[1:] + [None]):
        ahead = first(following) if following else None
        second(item, held)
        held = ahead


def attend(usable, queries, keys, values, routed):
    heads = queries.shape[1] // HD
    shares, rows = routed.shape[0], routed.shape[2]
    step = HEADS_A_STEP
    return pl.pallas_call(
        attend_kernel,
        grid_spec=pltpu.PrefetchScalarGridSpec(
            num_scalar_prefetch=1,
            grid=(heads // step,),
            in_specs=[
                pl.BlockSpec((BS, step * HD), lambda i, u: (0, i)),
                pl.BlockSpec((BS, HD), lambda i, u: (0, i * step // GROUP)),
                pl.BlockSpec((BS, HD), lambda i, u: (0, i * step // GROUP)),
                pl.BlockSpec((shares, 2, rows, 2 * HD), lambda i, u: (0, i * step // GROUP, 0, 0)),
            ],
            out_specs=pl.BlockSpec((BS, step * HD), lambda i, u: (0, i)),
        ),
        out_shape=jax.ShapeDtypeStruct(queries.shape, queries.dtype),
        compiler_params=pltpu.CompilerParams(vmem_limit_bytes=48 * 2**20),
        cost_estimate=pl.CostEstimate(
            flops=4 * BS * 3 * BS * HD * heads,
            bytes_accessed=4 * queries.size + 8 * keys.size,
            transcendentals=BS * 3 * BS * heads,
        ),
        name="attend",
    )(usable, queries, keys, values, routed)


def resident(queries, keys, values, chosen):
    count = lax.axis_size(AXES)
    me = lax.axis_index(AXES)
    kv_heads = keys.shape[1] // HD
    rows = BS // count
    pairs = jnp.concatenate(
        [keys.reshape(count, rows, kv_heads, HD), values.reshape(count, rows, kv_heads, HD)], axis=3
    )
    shared = lax.all_to_all(pairs.transpose(0, 2, 1, 3), AXES, 0, 0, tiled=True)
    table = shared.reshape(count * kv_heads, rows, 2 * HD)
    wanted = chosen * kv_heads + jnp.arange(kv_heads, dtype=jnp.int32)[None, :, None]
    request = table[wanted.reshape(-1)].reshape(count, kv_heads * 2, rows, 2 * HD)
    routed = lax.all_to_all(request, AXES, 0, 0, tiled=True)
    own_ids = lax.dynamic_index_in_dim(chosen, me, 0, keepdims=False)
    usable = (own_ids < me).astype(jnp.int32)
    return attend(usable, queries, keys, values, routed)


def as_sent(x):
    return jax.tree.map(lambda a: a.astype(jnp.bfloat16) if a.dtype == jnp.float32 else a, x)


def split_heads(queries, keys, values, chosen):
    scale = HD ** (-0.5)
    blk_count = lax.axis_size("blk")
    rank = lax.axis_index("blk")
    head = lax.axis_index("uly")
    tok = queries.shape[0]
    kv_heads = keys.shape[1] // HD
    q_split = queries.reshape(tok, kv_heads, GROUP * HD)
    kv_split = jnp.concatenate(
        [keys.reshape(tok, kv_heads, HD), values.reshape(tok, kv_heads, HD)], axis=2
    )
    q_head, kv_head = (
        lax.all_to_all(q_split, "uly", split_axis=1, concat_axis=0, tiled=True),
        lax.all_to_all(kv_split, "uly", split_axis=1, concat_axis=0, tiled=True),
    )
    span = q_head.shape[0]
    blocks_here = span // BS
    pieces = BS // blk_count
    spread = lax.all_to_all(
        kv_head.reshape(1, blocks_here, blk_count, pieces, 2 * HD),
        "blk",
        split_axis=2,
        concat_axis=0,
        tiled=True,
    )
    table = spread.reshape(blk_count * blocks_here, pieces, 2 * HD)
    wanted = lax.dynamic_index_in_dim(chosen, head, 1, keepdims=False)
    own_ids = lax.dynamic_slice_in_dim(wanted, rank * blocks_here, blocks_here, 0)
    block_ids = rank * blocks_here + jnp.arange(blocks_here, dtype=jnp.int32)
    usable = own_ids < block_ids[:, None]
    q_blocks = q_head.reshape(blocks_here, BS, GROUP, HD)
    own_rows = kv_head.reshape(blocks_here, BS, 2 * HD)
    causal = jnp.arange(BS, dtype=jnp.int32)[None, :] <= jnp.arange(BS, dtype=jnp.int32)[:, None]
    items = jnp.arange(blocks_here * GROUP, dtype=jnp.int32)
    contract = (((1,), (1,)), ((), ()))

    def query_of(item):
        block_q = lax.dynamic_index_in_dim(q_blocks, item // GROUP, 0, keepdims=False)
        return lax.dynamic_index_in_dim(block_q, item % GROUP, 1, keepdims=False)

    def own_part(item):
        query_rows = query_of(item)
        kv_rows = lax.dynamic_index_in_dim(own_rows, item // GROUP, 0, keepdims=False)
        scores = (
            lax.dot_general(
                query_rows, kv_rows[:, :HD], contract, preferred_element_type=jnp.float32
            )
            * scale
        )
        return jnp.where(causal, scores, -jnp.inf)

    def finish(item, own_scores, picked):
        index = item // GROUP
        query_rows = query_of(item)
        own_kv = lax.dynamic_index_in_dim(own_rows, index, 0, keepdims=False)
        routed_kv = lax.dynamic_index_in_dim(picked, index, 0, keepdims=False)
        allowed = lax.dynamic_index_in_dim(usable, index, 0, keepdims=False)
        routed_scores = (
            lax.dot_general(
                query_rows, routed_kv[:, :HD], contract, preferred_element_type=jnp.float32
            )
            * scale
        )
        routed_mask = jnp.repeat(allowed, BS, total_repeat_length=2 * BS)[None, :]
        routed_scores = jnp.where(routed_mask, routed_scores, -jnp.inf)
        top = jnp.maximum(jnp.max(own_scores, axis=-1), jnp.max(routed_scores, axis=-1))[:, None]
        own_weights = jnp.exp(own_scores - top)
        routed_weights = jnp.exp(routed_scores - top)
        total = jnp.sum(own_weights, axis=-1) + jnp.sum(routed_weights, axis=-1)
        summed = jnp.dot(
            own_weights.astype(jnp.bfloat16), own_kv[:, HD:], preferred_element_type=jnp.float32
        )
        summed = summed + jnp.dot(
            routed_weights.astype(jnp.bfloat16),
            routed_kv[:, HD:],
            preferred_element_type=jnp.float32,
        )
        return (summed / total[:, None]).astype(jnp.bfloat16)

    request = table[wanted.reshape(-1)].reshape(blk_count, blocks_here * 2, 1, pieces, 2 * HD)
    arrived = lax.all_to_all(request, "blk", split_axis=0, concat_axis=2, tiled=True)
    picked = arrived.reshape(blocks_here, 2 * BS, 2 * HD)

    def with_late(item):
        return finish(item, own_part(item), picked)

    result = lax.map(with_late, items)
    gathered = (
        result.reshape(blocks_here, GROUP, BS, HD)
        .transpose(0, 2, 1, 3)
        .reshape(span, 1, GROUP * HD)
    )
    returned = lax.all_to_all(
        as_sent(gathered), "uly", split_axis=0, concat_axis=1, tiled=True
    ).astype(gathered.dtype)
    return returned.reshape(tok, kv_heads * GROUP * HD)


def local(queries, keys, values, chosen):
    count = lax.axis_size(AXES)
    if queries.shape[0] == BS and BS % (16 * count) == 0:
        return resident(queries, keys, values, chosen)
    return split_heads(queries, keys, values, chosen)


def solution(mesh):
    placed = (P(("blk", "uly"), None), P(("blk", "uly"), None), P(("blk", "uly"), None), P())
    return jax.shard_map(
        local, mesh=mesh, in_specs=placed, out_specs=P(("blk", "uly"), None), check_vma=False
    )
```

```python
import functools
import math

import jax
import jax.numpy as jnp
from jax import lax
from jax.experimental import pallas as pl
from jax.experimental.pallas import tpu as pltpu
from jax.sharding import PartitionSpec as P

BS = 512
HD = 128
GROUP = 8
AXES = ("blk", "uly")
TILE = 256
STEP = GROUP
ROOM = 2.0**100
EXPONENT = HD ** (-0.5) * math.log2(math.e)


def scores_of(rows, key_rows):
    return lax.dot_general(
        rows, key_rows, (((1,), (1,)), ((), ())), preferred_element_type=jnp.float32
    )


def weighted(scores, top, values):
    weights = jnp.exp2(scores * EXPONENT - top).astype(jnp.bfloat16)
    return jnp.dot(weights, values, preferred_element_type=jnp.float32)


def lane_max(scores):
    parts = [scores[:, i : i + HD] for i in range(0, scores.shape[1], HD)]
    return functools.reduce(jnp.maximum, parts)


def staggered(items, first, second):
    held = first(items[0])
    for item, following in zip(items, items[1:] + [None]):
        ahead = first(following) if following else None
        second(item, held)
        held = ahead


def with_ones(values):
    return jnp.concatenate([values, jnp.ones_like(values)], axis=1)


def own_kernel(q_ref, k_ref, v_ref, sum_ref, stat_ref):
    keys = k_ref[...]
    values = with_ones(v_ref[...])
    shape = (TILE, TILE)
    causal = lax.broadcasted_iota(jnp.int32, shape, 1) <= lax.broadcasted_iota(jnp.int32, shape, 0)
    lane = lax.broadcasted_iota(jnp.int32, (TILE, HD), 1)
    stats = {}

    def first(item):
        h, start = item
        rows = q_ref[start : start + TILE, h * HD : (h + 1) * HD]
        return scores_of(rows, keys[: start + TILE])

    def second(item, scores):
        h, start = item
        diagonal = jnp.where(causal, scores[:, start:], -jnp.inf)
        scores = jnp.concatenate([scores[:, :start], diagonal], axis=1) if start else diagonal
        top = jnp.max(lane_max(scores), axis=1, keepdims=True) * EXPONENT
        both = weighted(scores, top, values[: start + TILE])
        sum_ref[start : start + TILE, h * HD : (h + 1) * HD] = both[:, :HD]
        stat = stats.get(start, jnp.zeros((TILE, HD), jnp.float32))
        stat = jnp.where(lane == h, top, stat)
        stats[start] = jnp.where(lane == STEP + h, both[:, HD:], stat)

    staggered([(h, t) for h in range(STEP) for t in range(0, BS, TILE)], first, second)
    for start, stat in stats.items():
        stat_ref[start : start + TILE, :] = stat


def attend_own(queries, keys, values):
    heads = queries.shape[1] // HD
    return pl.pallas_call(
        own_kernel,
        grid=(heads // STEP,),
        in_specs=[
            pl.BlockSpec((BS, STEP * HD), lambda i: (0, i)),
            pl.BlockSpec((BS, HD), lambda i: (0, i * STEP // GROUP)),
            pl.BlockSpec((BS, HD), lambda i: (0, i * STEP // GROUP)),
        ],
        out_specs=[
            pl.BlockSpec((BS, STEP * HD), lambda i: (0, i)),
            pl.BlockSpec((BS, HD), lambda i: (0, i)),
        ],
        out_shape=[
            jax.ShapeDtypeStruct(queries.shape, jnp.float32),
            jax.ShapeDtypeStruct((BS, heads // STEP * HD), jnp.float32),
        ],
        compiler_params=pltpu.CompilerParams(vmem_limit_bytes=48 * 2**20),
        cost_estimate=pl.CostEstimate(
            flops=3 * BS * BS * HD * heads,
            bytes_accessed=6 * queries.size,
            transcendentals=BS * BS * heads,
        ),
        name="attend_own",
    )(queries, keys, values)


def routed_kernel(usable, q_ref, first_key_ref, sum_ref, stat_ref, routed_ref, out_ref):
    kv_head = pl.program_id(0) * STEP // GROUP
    use = [usable[kv_head, s] != 0 for s in range(2)]
    none = jnp.zeros((), jnp.bfloat16)
    ones = jnp.ones((BS, HD), jnp.bfloat16)
    slots = range(2)
    keys = jnp.concatenate(
        [
            jnp.where(use[s], routed_ref[:, s, :, :HD].reshape(BS, HD), first_key_ref[0:1, :])
            for s in slots
        ],
        axis=0,
    )
    values = jnp.concatenate(
        [
            jnp.concatenate(
                [
                    jnp.where(use[s], routed_ref[:, s, :, HD:].reshape(BS, HD), none),
                    jnp.where(use[s], ones, none),
                ],
                axis=1,
            )
            for s in slots
        ],
        axis=0,
    )
    seen = []

    def first(item):
        h, start = item
        return scores_of(q_ref[start : start + TILE, h * HD : (h + 1) * HD], keys)

    def second(item, scores):
        h, start = item
        here = slice(start, start + TILE), slice(h * HD, (h + 1) * HD)
        own_top = stat_ref[start : start + TILE, h : h + 1]
        own_total = stat_ref[start : start + TILE, STEP + h : STEP + h + 1]
        both = weighted(scores, own_top, values)
        total = both[:, HD:] + own_total
        seen.append(total)
        out_ref[here] = ((both[:, :HD] + sum_ref[here]) / total).astype(out_ref.dtype)

    staggered([(h, t) for h in range(STEP) for t in range(0, BS, TILE)], first, second)
    in_range = functools.reduce(jnp.logical_and, [total < ROOM for total in seen])

    @pl.when(jnp.logical_not(jnp.all(in_range)))
    def _():
        lane = lax.broadcasted_iota(jnp.int32, (TILE, HD), 1)

        @pl.loop(0, STEP * (BS // TILE))
        def _(item):
            h = item // (BS // TILE)
            rows = pl.ds(pl.multiple_of(item % (BS // TILE) * TILE, TILE), TILE)
            here = rows, pl.ds(pl.multiple_of(h * HD, HD), HD)
            stat = stat_ref[rows, :]
            own_top = jnp.sum(jnp.where(lane == h, stat, 0.0), axis=1, keepdims=True)
            own_total = jnp.sum(jnp.where(lane == STEP + h, stat, 0.0), axis=1, keepdims=True)
            scores = scores_of(q_ref[here], keys)
            top = jnp.max(lane_max(scores), axis=1, keepdims=True) * EXPONENT
            top = jnp.maximum(top, own_top)
            scale = jnp.exp2(own_top - top)
            both = weighted(scores, top, values)
            total = both[:, HD:] + own_total * scale
            out_ref[here] = ((both[:, :HD] + sum_ref[here] * scale) / total).astype(out_ref.dtype)


def attend_routed(usable, queries, keys, own_sum, own_stat, routed):
    shares, _, rows, _ = routed.shape
    heads = queries.shape[1] // HD
    here = lambda i, u: (0, i)
    return pl.pallas_call(
        routed_kernel,
        grid_spec=pltpu.PrefetchScalarGridSpec(
            num_scalar_prefetch=1,
            grid=(heads // STEP,),
            in_specs=[
                pl.BlockSpec((BS, STEP * HD), here),
                pl.BlockSpec((16, HD), lambda i, u: (0, i * STEP // GROUP)),
                pl.BlockSpec((BS, STEP * HD), here),
                pl.BlockSpec((BS, HD), here),
                pl.BlockSpec((shares, 2, rows, 2 * HD), lambda i, u: (0, i * STEP // GROUP, 0, 0)),
            ],
            out_specs=pl.BlockSpec((BS, STEP * HD), here),
        ),
        out_shape=jax.ShapeDtypeStruct(queries.shape, queries.dtype),
        compiler_params=pltpu.CompilerParams(vmem_limit_bytes=48 * 2**20),
        cost_estimate=pl.CostEstimate(
            flops=8 * BS * BS * HD * heads,
            bytes_accessed=8 * BS * heads * HD + 2 * routed.size,
            transcendentals=2 * BS * BS * heads,
        ),
        name="attend_routed",
    )(usable, queries, keys, own_sum, own_stat, routed)


def pack_kernel(k_ref, v_ref, out_ref):
    shares, heads, rows, _ = out_ref.shape
    for h in range(heads):
        part = slice(h * HD, (h + 1) * HD)
        out_ref[:, h, :, :HD] = k_ref[:, part].reshape(shares, rows, HD)
        out_ref[:, h, :, HD:] = v_ref[:, part].reshape(shares, rows, HD)


def pack(keys, values, shares):
    shape = (shares, keys.shape[1] // HD, BS // shares, 2 * HD)
    return pl.pallas_call(
        pack_kernel, out_shape=jax.ShapeDtypeStruct(shape, keys.dtype), name="pack"
    )(keys, values)


def resident(queries, keys, values, chosen):
    count = lax.axis_size(AXES)
    me = lax.axis_index(AXES)
    kv_heads = keys.shape[1] // HD
    usable = (lax.dynamic_index_in_dim(chosen, me, 0, keepdims=False) < me).astype(jnp.int32)
    wanted = chosen * kv_heads + jnp.arange(kv_heads, dtype=jnp.int32)[None, :, None]
    table = lax.all_to_all(pack(keys, values, count), AXES, 0, 0, tiled=True)
    table = table.reshape(count * kv_heads, BS // count, 2 * HD)
    own_sum, own_stat = attend_own(queries, keys, values)
    wanted, own_stat = lax.optimization_barrier((wanted.reshape(-1), own_stat))
    request = table[wanted].reshape(count, kv_heads * 2, BS // count, 2 * HD)
    routed = lax.all_to_all(request, AXES, 0, 0, tiled=True)
    return attend_routed(usable, queries, keys, own_sum, own_stat, routed)


def as_sent(x):
    return jax.tree.map(lambda a: a.astype(jnp.bfloat16) if a.dtype == jnp.float32 else a, x)


def split_heads(queries, keys, values, chosen):
    scale = HD ** (-0.5)
    blk_count = lax.axis_size("blk")
    rank = lax.axis_index("blk")
    head = lax.axis_index("uly")
    tok = queries.shape[0]
    kv_heads = keys.shape[1] // HD
    q_split = queries.reshape(tok, kv_heads, GROUP * HD)
    kv_split = jnp.concatenate(
        [keys.reshape(tok, kv_heads, HD), values.reshape(tok, kv_heads, HD)], axis=2
    )
    q_head, kv_head = (
        lax.all_to_all(q_split, "uly", split_axis=1, concat_axis=0, tiled=True),
        lax.all_to_all(kv_split, "uly", split_axis=1, concat_axis=0, tiled=True),
    )
    span = q_head.shape[0]
    blocks_here = span // BS
    pieces = BS // blk_count
    spread = lax.all_to_all(
        kv_head.reshape(1, blocks_here, blk_count, pieces, 2 * HD),
        "blk",
        split_axis=2,
        concat_axis=0,
        tiled=True,
    )
    table = spread.reshape(blk_count * blocks_here, pieces, 2 * HD)
    wanted = lax.dynamic_index_in_dim(chosen, head, 1, keepdims=False)
    own_ids = lax.dynamic_slice_in_dim(wanted, rank * blocks_here, blocks_here, 0)
    block_ids = rank * blocks_here + jnp.arange(blocks_here, dtype=jnp.int32)
    usable = own_ids < block_ids[:, None]
    q_blocks = q_head.reshape(blocks_here, BS, GROUP, HD)
    own_rows = kv_head.reshape(blocks_here, BS, 2 * HD)
    causal = jnp.arange(BS, dtype=jnp.int32)[None, :] <= jnp.arange(BS, dtype=jnp.int32)[:, None]
    items = jnp.arange(blocks_here * GROUP, dtype=jnp.int32)
    contract = (((1,), (1,)), ((), ()))

    def query_of(item):
        block_q = lax.dynamic_index_in_dim(q_blocks, item // GROUP, 0, keepdims=False)
        return lax.dynamic_index_in_dim(block_q, item % GROUP, 1, keepdims=False)

    def own_part(item):
        query_rows = query_of(item)
        kv_rows = lax.dynamic_index_in_dim(own_rows, item // GROUP, 0, keepdims=False)
        scores = (
            lax.dot_general(
                query_rows, kv_rows[:, :HD], contract, preferred_element_type=jnp.float32
            )
            * scale
        )
        return jnp.where(causal, scores, -jnp.inf)

    def finish(item, own_scores, picked):
        index = item // GROUP
        query_rows = query_of(item)
        own_kv = lax.dynamic_index_in_dim(own_rows, index, 0, keepdims=False)
        routed_kv = lax.dynamic_index_in_dim(picked, index, 0, keepdims=False)
        allowed = lax.dynamic_index_in_dim(usable, index, 0, keepdims=False)
        routed_scores = (
            lax.dot_general(
                query_rows, routed_kv[:, :HD], contract, preferred_element_type=jnp.float32
            )
            * scale
        )
        routed_mask = jnp.repeat(allowed, BS, total_repeat_length=2 * BS)[None, :]
        routed_scores = jnp.where(routed_mask, routed_scores, -jnp.inf)
        top = jnp.maximum(jnp.max(own_scores, axis=-1), jnp.max(routed_scores, axis=-1))[:, None]
        own_weights = jnp.exp(own_scores - top)
        routed_weights = jnp.exp(routed_scores - top)
        total = jnp.sum(own_weights, axis=-1) + jnp.sum(routed_weights, axis=-1)
        summed = jnp.dot(
            own_weights.astype(jnp.bfloat16), own_kv[:, HD:], preferred_element_type=jnp.float32
        )
        summed = summed + jnp.dot(
            routed_weights.astype(jnp.bfloat16),
            routed_kv[:, HD:],
            preferred_element_type=jnp.float32,
        )
        return (summed / total[:, None]).astype(jnp.bfloat16)

    request = table[wanted.reshape(-1)].reshape(blk_count, blocks_here * 2, 1, pieces, 2 * HD)
    arrived = lax.all_to_all(request, "blk", split_axis=0, concat_axis=2, tiled=True)
    picked = arrived.reshape(blocks_here, 2 * BS, 2 * HD)

    def with_late(item):
        return finish(item, own_part(item), picked)

    result = lax.map(with_late, items)
    gathered = (
        result.reshape(blocks_here, GROUP, BS, HD)
        .transpose(0, 2, 1, 3)
        .reshape(span, 1, GROUP * HD)
    )
    returned = lax.all_to_all(
        as_sent(gathered), "uly", split_axis=0, concat_axis=1, tiled=True
    ).astype(gathered.dtype)
    return returned.reshape(tok, kv_heads * GROUP * HD)


def local(queries, keys, values, chosen):
    count = lax.axis_size(AXES)
    if queries.shape[0] == BS and BS % (16 * count) == 0:
        return resident(queries, keys, values, chosen)
    return split_heads(queries, keys, values, chosen)


def solution(mesh):
    placed = (P(AXES, None), P(AXES, None), P(AXES, None), P())
    return jax.shard_map(
        local, mesh=mesh, in_specs=placed, out_specs=P(AXES, None), check_vma=False
    )
```

```python
import functools
import math

import jax
import jax.numpy as jnp
from jax import lax
from jax.experimental import pallas as pl
from jax.experimental.pallas import tpu as pltpu
from jax.sharding import PartitionSpec as P

BS = 512
HD = 128
GROUP = 8
AXES = ("blk", "uly")
TILE = 256
STEP = GROUP
ROOM = 2.0**100
EXPONENT = HD ** (-0.5) * math.log2(math.e)


def scores_of(key_rows, rows):
    return lax.dot_general(
        key_rows, rows, (((1,), (1,)), ((), ())), preferred_element_type=jnp.float32
    )


def weighted(values, scores, top):
    weights = jnp.exp2(scores * EXPONENT - top).astype(jnp.bfloat16)
    both = jnp.dot(values, weights, preferred_element_type=jnp.float32)
    return both[:HD], both[HD : HD + 1]


def over_ones(values, ones):
    return jnp.concatenate([values.T, ones], axis=0)


def staggered(items, first, second):
    held = first(items[0])
    for item, following in zip(items, items[1:] + [None]):
        ahead = first(following) if following else None
        second(item, held)
        held = ahead


def own_kernel(q_ref, k_ref, v_ref, sum_ref, stat_ref):
    keys = k_ref[...]
    values = over_ones(v_ref[...], jnp.ones((16, BS), jnp.bfloat16))
    shape = (TILE, TILE)
    causal = lax.broadcasted_iota(jnp.int32, shape, 0) <= lax.broadcasted_iota(jnp.int32, shape, 1)

    def first(item):
        h, start = item
        rows = q_ref[start : start + TILE, h * HD : (h + 1) * HD]
        return scores_of(keys[: start + TILE], rows)

    def second(item, scores):
        h, start = item
        here = slice(start, start + TILE)
        diagonal = jnp.where(causal, scores[start:], -jnp.inf)
        scores = jnp.concatenate([scores[:start], diagonal], axis=0) if start else diagonal
        top = jnp.max(scores, axis=0, keepdims=True) * EXPONENT
        summed, total = weighted(values[:, : start + TILE], scores, top)
        sum_ref[h * HD : (h + 1) * HD, here] = summed
        stat_ref[h : h + 1, here] = top
        stat_ref[STEP + h : STEP + h + 1, here] = total

    staggered([(h, t) for h in range(STEP) for t in range(0, BS, TILE)], first, second)


def attend_own(queries, keys, values):
    heads = queries.shape[1] // HD
    return pl.pallas_call(
        own_kernel,
        grid=(heads // STEP,),
        in_specs=[
            pl.BlockSpec((BS, STEP * HD), lambda i: (0, i)),
            pl.BlockSpec((BS, HD), lambda i: (0, i * STEP // GROUP)),
            pl.BlockSpec((BS, HD), lambda i: (0, i * STEP // GROUP)),
        ],
        out_specs=[
            pl.BlockSpec((STEP * HD, BS), lambda i: (i, 0)),
            pl.BlockSpec((2 * STEP, BS), lambda i: (i, 0)),
        ],
        out_shape=[
            jax.ShapeDtypeStruct((heads * HD, BS), jnp.float32),
            jax.ShapeDtypeStruct((heads * 2, BS), jnp.float32),
        ],
        compiler_params=pltpu.CompilerParams(vmem_limit_bytes=48 * 2**20),
        cost_estimate=pl.CostEstimate(
            flops=3 * BS * BS * HD * heads,
            bytes_accessed=6 * queries.size,
            transcendentals=BS * BS * heads,
        ),
        name="attend_own",
    )(queries, keys, values)


def routed_kernel(usable, q_ref, first_key_ref, sum_ref, stat_ref, routed_ref, out_ref):
    kv_head = pl.program_id(0) * STEP // GROUP
    use = [usable[kv_head, s] != 0 for s in range(2)]
    none = jnp.zeros((), jnp.bfloat16)
    slots = range(2)
    keys = jnp.concatenate(
        [
            jnp.where(use[s], routed_ref[:, s, :, :HD].reshape(BS, HD), first_key_ref[0:1, :])
            for s in slots
        ],
        axis=0,
    )
    values = jnp.concatenate(
        [jnp.where(use[s], routed_ref[:, s, :, HD:].reshape(BS, HD), none) for s in slots], axis=0
    )
    ones = jnp.ones((16, BS), jnp.bfloat16)
    ones = jnp.concatenate([jnp.where(use[s], ones, none) for s in slots], axis=1)
    values = over_ones(values, ones)
    seen = []

    def first(item):
        h, start = item
        return scores_of(keys, q_ref[start : start + TILE, h * HD : (h + 1) * HD])

    def second(item, scores):
        h, start = item
        rows, part = slice(start, start + TILE), slice(h * HD, (h + 1) * HD)
        summed, total = weighted(values, scores, stat_ref[h : h + 1, rows])
        total = total + stat_ref[STEP + h : STEP + h + 1, rows]
        seen.append(total)
        summed = (summed + sum_ref[part, rows]) / total
        out_ref[rows, part] = summed.astype(out_ref.dtype).T

    staggered([(h, t) for h in range(STEP) for t in range(0, BS, TILE)], first, second)
    in_range = functools.reduce(jnp.logical_and, [total < ROOM for total in seen])

    @pl.when(jnp.logical_not(jnp.all(in_range)))
    def _():
        @pl.loop(0, STEP)
        def _(h):
            part = pl.ds(pl.multiple_of(h * HD, HD), HD)
            for start in range(0, BS, TILE):
                rows = slice(start, start + TILE)
                own_top = stat_ref[pl.ds(h, 1), rows]
                own_total = stat_ref[pl.ds(STEP + h, 1), rows]
                scores = scores_of(keys, q_ref[rows, part])
                top = jnp.max(scores, axis=0, keepdims=True) * EXPONENT
                top = jnp.maximum(top, own_top)
                scale = jnp.exp2(own_top - top)
                summed, total = weighted(values, scores, top)
                summed = (summed + sum_ref[part, rows] * scale) / (total + own_total * scale)
                out_ref[rows, part] = summed.astype(out_ref.dtype).T


def attend_routed(usable, queries, keys, own_sum, own_stat, routed):
    shares, _, rows, _ = routed.shape
    heads = queries.shape[1] // HD
    return pl.pallas_call(
        routed_kernel,
        grid_spec=pltpu.PrefetchScalarGridSpec(
            num_scalar_prefetch=1,
            grid=(heads // STEP,),
            in_specs=[
                pl.BlockSpec((BS, STEP * HD), lambda i, u: (0, i)),
                pl.BlockSpec((16, HD), lambda i, u: (0, i * STEP // GROUP)),
                pl.BlockSpec((STEP * HD, BS), lambda i, u: (i, 0)),
                pl.BlockSpec((2 * STEP, BS), lambda i, u: (i, 0)),
                pl.BlockSpec((shares, 2, rows, 2 * HD), lambda i, u: (0, i * STEP // GROUP, 0, 0)),
            ],
            out_specs=pl.BlockSpec((BS, STEP * HD), lambda i, u: (0, i)),
        ),
        out_shape=jax.ShapeDtypeStruct(queries.shape, queries.dtype),
        compiler_params=pltpu.CompilerParams(vmem_limit_bytes=48 * 2**20),
        cost_estimate=pl.CostEstimate(
            flops=8 * BS * BS * HD * heads,
            bytes_accessed=8 * BS * heads * HD + 2 * routed.size,
            transcendentals=2 * BS * BS * heads,
        ),
        name="attend_routed",
    )(usable, queries, keys, own_sum, own_stat, routed)


def pack_kernel(k_ref, v_ref, out_ref):
    shares, heads, rows, _ = out_ref.shape
    for h in range(heads):
        part = slice(h * HD, (h + 1) * HD)
        out_ref[:, h, :, :HD] = k_ref[:, part].reshape(shares, rows, HD)
        out_ref[:, h, :, HD:] = v_ref[:, part].reshape(shares, rows, HD)


def pack(keys, values, shares):
    shape = (shares, keys.shape[1] // HD, BS // shares, 2 * HD)
    return pl.pallas_call(
        pack_kernel, out_shape=jax.ShapeDtypeStruct(shape, keys.dtype), name="pack"
    )(keys, values)


def resident(queries, keys, values, chosen):
    count = lax.axis_size(AXES)
    me = lax.axis_index(AXES)
    kv_heads = keys.shape[1] // HD
    usable = (lax.dynamic_index_in_dim(chosen, me, 0, keepdims=False) < me).astype(jnp.int32)
    wanted = chosen * kv_heads + jnp.arange(kv_heads, dtype=jnp.int32)[None, :, None]
    table = lax.all_to_all(pack(keys, values, count), AXES, 0, 0, tiled=True)
    table = table.reshape(count * kv_heads, BS // count, 2 * HD)
    own_sum, own_stat = attend_own(queries, keys, values)
    wanted, own_stat = lax.optimization_barrier((wanted.reshape(-1), own_stat))
    request = table[wanted].reshape(count, kv_heads * 2, BS // count, 2 * HD)
    routed = lax.all_to_all(request, AXES, 0, 0, tiled=True)
    return attend_routed(usable, queries, keys, own_sum, own_stat, routed)


def as_sent(x):
    return jax.tree.map(lambda a: a.astype(jnp.bfloat16) if a.dtype == jnp.float32 else a, x)


def split_heads(queries, keys, values, chosen):
    scale = HD ** (-0.5)
    blk_count = lax.axis_size("blk")
    rank = lax.axis_index("blk")
    head = lax.axis_index("uly")
    tok = queries.shape[0]
    kv_heads = keys.shape[1] // HD
    q_split = queries.reshape(tok, kv_heads, GROUP * HD)
    kv_split = jnp.concatenate(
        [keys.reshape(tok, kv_heads, HD), values.reshape(tok, kv_heads, HD)], axis=2
    )
    q_head, kv_head = (
        lax.all_to_all(q_split, "uly", split_axis=1, concat_axis=0, tiled=True),
        lax.all_to_all(kv_split, "uly", split_axis=1, concat_axis=0, tiled=True),
    )
    span = q_head.shape[0]
    blocks_here = span // BS
    pieces = BS // blk_count
    spread = lax.all_to_all(
        kv_head.reshape(1, blocks_here, blk_count, pieces, 2 * HD),
        "blk",
        split_axis=2,
        concat_axis=0,
        tiled=True,
    )
    table = spread.reshape(blk_count * blocks_here, pieces, 2 * HD)
    wanted = lax.dynamic_index_in_dim(chosen, head, 1, keepdims=False)
    own_ids = lax.dynamic_slice_in_dim(wanted, rank * blocks_here, blocks_here, 0)
    block_ids = rank * blocks_here + jnp.arange(blocks_here, dtype=jnp.int32)
    usable = own_ids < block_ids[:, None]
    q_blocks = q_head.reshape(blocks_here, BS, GROUP, HD)
    own_rows = kv_head.reshape(blocks_here, BS, 2 * HD)
    causal = jnp.arange(BS, dtype=jnp.int32)[None, :] <= jnp.arange(BS, dtype=jnp.int32)[:, None]
    items = jnp.arange(blocks_here * GROUP, dtype=jnp.int32)
    contract = (((1,), (1,)), ((), ()))

    def query_of(item):
        block_q = lax.dynamic_index_in_dim(q_blocks, item // GROUP, 0, keepdims=False)
        return lax.dynamic_index_in_dim(block_q, item % GROUP, 1, keepdims=False)

    def own_part(item):
        query_rows = query_of(item)
        kv_rows = lax.dynamic_index_in_dim(own_rows, item // GROUP, 0, keepdims=False)
        scores = (
            lax.dot_general(
                query_rows, kv_rows[:, :HD], contract, preferred_element_type=jnp.float32
            )
            * scale
        )
        return jnp.where(causal, scores, -jnp.inf)

    def finish(item, own_scores, picked):
        index = item // GROUP
        query_rows = query_of(item)
        own_kv = lax.dynamic_index_in_dim(own_rows, index, 0, keepdims=False)
        routed_kv = lax.dynamic_index_in_dim(picked, index, 0, keepdims=False)
        allowed = lax.dynamic_index_in_dim(usable, index, 0, keepdims=False)
        routed_scores = (
            lax.dot_general(
                query_rows, routed_kv[:, :HD], contract, preferred_element_type=jnp.float32
            )
            * scale
        )
        routed_mask = jnp.repeat(allowed, BS, total_repeat_length=2 * BS)[None, :]
        routed_scores = jnp.where(routed_mask, routed_scores, -jnp.inf)
        top = jnp.maximum(jnp.max(own_scores, axis=-1), jnp.max(routed_scores, axis=-1))[:, None]
        own_weights = jnp.exp(own_scores - top)
        routed_weights = jnp.exp(routed_scores - top)
        total = jnp.sum(own_weights, axis=-1) + jnp.sum(routed_weights, axis=-1)
        summed = jnp.dot(
            own_weights.astype(jnp.bfloat16), own_kv[:, HD:], preferred_element_type=jnp.float32
        )
        summed = summed + jnp.dot(
            routed_weights.astype(jnp.bfloat16),
            routed_kv[:, HD:],
            preferred_element_type=jnp.float32,
        )
        return (summed / total[:, None]).astype(jnp.bfloat16)

    request = table[wanted.reshape(-1)].reshape(blk_count, blocks_here * 2, 1, pieces, 2 * HD)
    arrived = lax.all_to_all(request, "blk", split_axis=0, concat_axis=2, tiled=True)
    picked = arrived.reshape(blocks_here, 2 * BS, 2 * HD)

    def with_late(item):
        return finish(item, own_part(item), picked)

    result = lax.map(with_late, items)
    gathered = (
        result.reshape(blocks_here, GROUP, BS, HD)
        .transpose(0, 2, 1, 3)
        .reshape(span, 1, GROUP * HD)
    )
    returned = lax.all_to_all(
        as_sent(gathered), "uly", split_axis=0, concat_axis=1, tiled=True
    ).astype(gathered.dtype)
    return returned.reshape(tok, kv_heads * GROUP * HD)


def local(queries, keys, values, chosen):
    count = lax.axis_size(AXES)
    if queries.shape[0] == BS and BS % (16 * count) == 0:
        return resident(queries, keys, values, chosen)
    return split_heads(queries, keys, values, chosen)


def solution(mesh):
    placed = (P(AXES, None), P(AXES, None), P(AXES, None), P())
    return jax.shard_map(
        local, mesh=mesh, in_specs=placed, out_specs=P(AXES, None), check_vma=False
    )
```

```python
import functools
import math

import jax
import jax.numpy as jnp
from jax import lax
from jax.experimental import pallas as pl
from jax.experimental.pallas import tpu as pltpu
from jax.sharding import PartitionSpec as P

BS = 512
HD = 128
GROUP = 8
AXES = ("blk", "uly")
TILE = 256
CHUNK = 256
EARLY = 4
CUT = 12
STEP = GROUP
ROOM = 2.0**100
EXPONENT = HD ** (-0.5) * math.log2(math.e)


def scores_of(key_rows, rows):
    return lax.dot_general(
        key_rows, rows, (((1,), (1,)), ((), ())), preferred_element_type=jnp.float32
    )


def weighted(values, scores, top):
    weights = jnp.exp2(scores * EXPONENT - top).astype(jnp.bfloat16)
    both = jnp.dot(values, weights, preferred_element_type=jnp.float32)
    return both[:HD], both[HD : HD + 1]


def over_ones(values, ones):
    return jnp.concatenate([values.T, ones], axis=0)


def staggered(items, first, second):
    held = first(items[0])
    for item, following in zip(items, items[1:] + [None]):
        ahead = first(following) if following else None
        second(item, held)
        held = ahead


def own_kernel(q_ref, k_ref, v_ref, sum_ref, stat_ref):
    keys = k_ref[...]
    values = over_ones(v_ref[...], jnp.ones((16, BS), jnp.bfloat16))
    shape = (TILE, TILE)
    causal = lax.broadcasted_iota(jnp.int32, shape, 0) <= lax.broadcasted_iota(jnp.int32, shape, 1)

    def first(item):
        h, start = item
        rows = q_ref[start : start + TILE, h * HD : (h + 1) * HD]
        return scores_of(keys[: start + TILE], rows)

    def second(item, scores):
        h, start = item
        here = slice(start, start + TILE)
        diagonal = jnp.where(causal, scores[start:], -jnp.inf)
        scores = jnp.concatenate([scores[:start], diagonal], axis=0) if start else diagonal
        top = jnp.max(scores, axis=0, keepdims=True) * EXPONENT
        summed, total = weighted(values[:, : start + TILE], scores, top)
        sum_ref[h * HD : (h + 1) * HD, here] = summed
        stat_ref[h : h + 1, here] = top
        stat_ref[STEP + h : STEP + h + 1, here] = total

    staggered([(h, t) for h in range(STEP) for t in range(0, BS, TILE)], first, second)


def attend_own(queries, keys, values):
    heads = queries.shape[1] // HD
    return pl.pallas_call(
        own_kernel,
        grid=(heads // STEP,),
        in_specs=[
            pl.BlockSpec((BS, STEP * HD), lambda i: (0, i)),
            pl.BlockSpec((BS, HD), lambda i: (0, i * STEP // GROUP)),
            pl.BlockSpec((BS, HD), lambda i: (0, i * STEP // GROUP)),
        ],
        out_specs=[
            pl.BlockSpec((STEP * HD, BS), lambda i: (i, 0)),
            pl.BlockSpec((2 * STEP, BS), lambda i: (i, 0)),
        ],
        out_shape=[
            jax.ShapeDtypeStruct((heads * HD, BS), jnp.float32),
            jax.ShapeDtypeStruct((heads * 2, BS), jnp.float32),
        ],
        compiler_params=pltpu.CompilerParams(vmem_limit_bytes=48 * 2**20),
        cost_estimate=pl.CostEstimate(
            flops=3 * BS * BS * HD * heads,
            bytes_accessed=6 * queries.size,
            transcendentals=BS * BS * heads,
        ),
        name="attend_own",
    )(queries, keys, values)


def routed_kernel(
    usable, q_ref, first_key_ref, sum_hbm, stat_ref, routed_ref, out_hbm, *scratch
):
    sum_ref, part_ref, total_ref, out_ref, sum_sem, out_sems = scratch
    bring = pltpu.make_async_copy(sum_hbm, sum_ref, sum_sem)
    bring.start()
    kv_heads = first_key_ref.shape[1] // HD
    heads = kv_heads * GROUP
    none = jnp.zeros((), jnp.bfloat16)
    ones = jnp.ones((16, BS), jnp.bfloat16)
    keys, values = {}, {}
    for g in range(kv_heads):
        for s in range(2):
            use = usable[g, s] != 0
            some, first_key = routed_ref[:, 2 * g + s], first_key_ref[0:1, g * HD : (g + 1) * HD]
            keys[g, s] = jnp.where(use, some[:, :, :HD].reshape(BS, HD), first_key)
            values[g, s] = over_ones(
                jnp.where(use, some[:, :, HD:].reshape(BS, HD), none), jnp.where(use, ones, none)
            )
    chunks = [(s, c) for s in range(2) for c in range(0, BS, CHUNK)]
    seen = []

    def columns(head, count):
        return pl.ds(head * HD, count * HD)

    def take_out(n, head, count):
        part = columns(head, count)
        return pltpu.make_async_copy(out_ref.at[:, part], out_hbm.at[:, part], out_sems.at[n])

    def stat_rows(h):
        own = h // GROUP * 2 * GROUP + h % GROUP
        return pl.ds(own, 1), pl.ds(GROUP + own, 1)

    def first(item):
        h, start = item
        rows = q_ref[start : start + TILE, h * HD : (h + 1) * HD]
        return [scores_of(keys[h // GROUP, s][c : c + CHUNK], rows) for s, c in chunks]

    def finish(item, summed, total):
        h, start = item
        rows, part = slice(start, start + TILE), columns(h, 1)
        summed = (summed + sum_ref[part, rows]) / total
        out_ref[rows, part] = summed.astype(out_ref.dtype).T

    def second(item, scores):
        h, start = item
        rows = slice(start, start + TILE)
        own_top, own_total = stat_rows(h)
        summed, total = 0.0, stat_ref[own_total, rows]
        for (s, c), some in zip(chunks, scores):
            more = weighted(values[h // GROUP, s][:, c : c + CHUNK], some, stat_ref[own_top, rows])
            summed, total = summed + more[0], total + more[1]
        seen.append(total)
        if h >= EARLY:
            finish(item, summed, total)
            if h == CUT - 1 and start == BS - TILE:
                take_out(0, 0, CUT).start()
            return
        part_ref[columns(h, 1), rows] = summed
        total_ref[h : h + 1, rows] = total
        if h == EARLY - 1 and start == BS - TILE:
            bring.wait()
            for h in range(EARLY):
                for start in range(0, BS, TILE):
                    rows = slice(start, start + TILE)
                    finish((h, start), part_ref[columns(h, 1), rows], total_ref[h : h + 1, rows])

    staggered([(h, t) for h in range(heads) for t in range(0, BS, TILE)], first, second)
    take_out(1, CUT, heads - CUT).start()
    take_out(0, 0, CUT).wait()
    take_out(1, CUT, heads - CUT).wait()
    in_range = functools.reduce(jnp.logical_and, [total < ROOM for total in seen])

    @pl.when(jnp.logical_not(jnp.all(in_range)))
    def _():
        for g in range(kv_heads):
            all_keys = jnp.concatenate([keys[g, s] for s in range(2)], axis=0)
            all_values = jnp.concatenate([values[g, s] for s in range(2)], axis=1)

            @pl.loop(g * GROUP, (g + 1) * GROUP)
            def _(h):
                part = pl.ds(pl.multiple_of(h * HD, HD), HD)
                for start in range(0, BS, TILE):
                    rows = slice(start, start + TILE)
                    own_top, own_total = [stat_ref[at, rows] for at in stat_rows(h)]
                    scores = scores_of(all_keys, q_ref[rows, part])
                    top = jnp.max(scores, axis=0, keepdims=True) * EXPONENT
                    top = jnp.maximum(top, own_top)
                    scale = jnp.exp2(own_top - top)
                    summed, total = weighted(all_values, scores, top)
                    summed = summed + sum_ref[part, rows] * scale
                    total = total + own_total * scale
                    out_ref[rows, part] = (summed / total).astype(out_ref.dtype).T

        again = take_out(0, 0, heads)
        again.start()
        again.wait()


def attend_routed(usable, queries, keys, own_sum, own_stat, routed):
    heads = queries.shape[1] // HD
    vmem, hbm = pl.BlockSpec(memory_space=pltpu.VMEM), pl.BlockSpec(memory_space=pltpu.HBM)
    return pl.pallas_call(
        routed_kernel,
        in_specs=[pl.BlockSpec(memory_space=pltpu.SMEM), vmem, vmem, hbm, vmem, vmem],
        out_specs=hbm,
        out_shape=jax.ShapeDtypeStruct(queries.shape, queries.dtype),
        scratch_shapes=[
            pltpu.VMEM(own_sum.shape, own_sum.dtype),
            pltpu.VMEM((EARLY * HD, BS), jnp.float32),
            pltpu.VMEM((8, BS), jnp.float32),
            pltpu.VMEM(queries.shape, queries.dtype),
            pltpu.SemaphoreType.DMA,
            pltpu.SemaphoreType.DMA((2,)),
        ],
        compiler_params=pltpu.CompilerParams(vmem_limit_bytes=32 * 2**20),
        cost_estimate=pl.CostEstimate(
            flops=8 * BS * BS * HD * heads,
            bytes_accessed=8 * BS * heads * HD + 2 * routed.size,
            transcendentals=2 * BS * BS * heads,
        ),
        name="attend_routed",
    )(usable, queries, keys, pltpu.with_memory_space_constraint(own_sum, pltpu.HBM), own_stat, routed)


def pack_kernel(k_ref, v_ref, out_ref):
    shares, heads, rows, _ = out_ref.shape
    for h in range(heads):
        part = slice(h * HD, (h + 1) * HD)
        out_ref[:, h, :, :HD] = k_ref[:, part].reshape(shares, rows, HD)
        out_ref[:, h, :, HD:] = v_ref[:, part].reshape(shares, rows, HD)


def pack(keys, values, shares):
    shape = (shares, keys.shape[1] // HD, BS // shares, 2 * HD)
    return pl.pallas_call(
        pack_kernel, out_shape=jax.ShapeDtypeStruct(shape, keys.dtype), name="pack"
    )(keys, values)


def resident(queries, keys, values, chosen):
    count = lax.axis_size(AXES)
    me = lax.axis_index(AXES)
    kv_heads = keys.shape[1] // HD
    usable = (lax.dynamic_index_in_dim(chosen, me, 0, keepdims=False) < me).astype(jnp.int32)
    wanted = chosen * kv_heads + jnp.arange(kv_heads, dtype=jnp.int32)[None, :, None]
    table = lax.all_to_all(pack(keys, values, count), AXES, 0, 0, tiled=True)
    table = table.reshape(count * kv_heads, BS // count, 2 * HD)
    own_sum, own_stat = attend_own(queries, keys, values)
    wanted, own_stat = lax.optimization_barrier((wanted.reshape(-1), own_stat))
    request = table[wanted].reshape(count, kv_heads * 2, BS // count, 2 * HD)
    routed = lax.all_to_all(request, AXES, 0, 0, tiled=True)
    return attend_routed(usable, queries, keys, own_sum, own_stat, routed)


def as_sent(x):
    return jax.tree.map(lambda a: a.astype(jnp.bfloat16) if a.dtype == jnp.float32 else a, x)


def split_heads(queries, keys, values, chosen):
    scale = HD ** (-0.5)
    blk_count = lax.axis_size("blk")
    rank = lax.axis_index("blk")
    head = lax.axis_index("uly")
    tok = queries.shape[0]
    kv_heads = keys.shape[1] // HD
    q_split = queries.reshape(tok, kv_heads, GROUP * HD)
    kv_split = jnp.concatenate(
        [keys.reshape(tok, kv_heads, HD), values.reshape(tok, kv_heads, HD)], axis=2
    )
    q_head, kv_head = (
        lax.all_to_all(q_split, "uly", split_axis=1, concat_axis=0, tiled=True),
        lax.all_to_all(kv_split, "uly", split_axis=1, concat_axis=0, tiled=True),
    )
    span = q_head.shape[0]
    blocks_here = span // BS
    pieces = BS // blk_count
    spread = lax.all_to_all(
        kv_head.reshape(1, blocks_here, blk_count, pieces, 2 * HD),
        "blk",
        split_axis=2,
        concat_axis=0,
        tiled=True,
    )
    table = spread.reshape(blk_count * blocks_here, pieces, 2 * HD)
    wanted = lax.dynamic_index_in_dim(chosen, head, 1, keepdims=False)
    own_ids = lax.dynamic_slice_in_dim(wanted, rank * blocks_here, blocks_here, 0)
    block_ids = rank * blocks_here + jnp.arange(blocks_here, dtype=jnp.int32)
    usable = own_ids < block_ids[:, None]
    q_blocks = q_head.reshape(blocks_here, BS, GROUP, HD)
    own_rows = kv_head.reshape(blocks_here, BS, 2 * HD)
    causal = jnp.arange(BS, dtype=jnp.int32)[None, :] <= jnp.arange(BS, dtype=jnp.int32)[:, None]
    items = jnp.arange(blocks_here * GROUP, dtype=jnp.int32)
    contract = (((1,), (1,)), ((), ()))

    def query_of(item):
        block_q = lax.dynamic_index_in_dim(q_blocks, item // GROUP, 0, keepdims=False)
        return lax.dynamic_index_in_dim(block_q, item % GROUP, 1, keepdims=False)

    def own_part(item):
        query_rows = query_of(item)
        kv_rows = lax.dynamic_index_in_dim(own_rows, item // GROUP, 0, keepdims=False)
        scores = (
            lax.dot_general(
                query_rows, kv_rows[:, :HD], contract, preferred_element_type=jnp.float32
            )
            * scale
        )
        return jnp.where(causal, scores, -jnp.inf)

    def finish(item, own_scores, picked):
        index = item // GROUP
        query_rows = query_of(item)
        own_kv = lax.dynamic_index_in_dim(own_rows, index, 0, keepdims=False)
        routed_kv = lax.dynamic_index_in_dim(picked, index, 0, keepdims=False)
        allowed = lax.dynamic_index_in_dim(usable, index, 0, keepdims=False)
        routed_scores = (
            lax.dot_general(
                query_rows, routed_kv[:, :HD], contract, preferred_element_type=jnp.float32
            )
            * scale
        )
        routed_mask = jnp.repeat(allowed, BS, total_repeat_length=2 * BS)[None, :]
        routed_scores = jnp.where(routed_mask, routed_scores, -jnp.inf)
        top = jnp.maximum(jnp.max(own_scores, axis=-1), jnp.max(routed_scores, axis=-1))[:, None]
        own_weights = jnp.exp(own_scores - top)
        routed_weights = jnp.exp(routed_scores - top)
        total = jnp.sum(own_weights, axis=-1) + jnp.sum(routed_weights, axis=-1)
        summed = jnp.dot(
            own_weights.astype(jnp.bfloat16), own_kv[:, HD:], preferred_element_type=jnp.float32
        )
        summed = summed + jnp.dot(
            routed_weights.astype(jnp.bfloat16),
            routed_kv[:, HD:],
            preferred_element_type=jnp.float32,
        )
        return (summed / total[:, None]).astype(jnp.bfloat16)

    request = table[wanted.reshape(-1)].reshape(blk_count, blocks_here * 2, 1, pieces, 2 * HD)
    arrived = lax.all_to_all(request, "blk", split_axis=0, concat_axis=2, tiled=True)
    picked = arrived.reshape(blocks_here, 2 * BS, 2 * HD)

    def with_late(item):
        return finish(item, own_part(item), picked)

    result = lax.map(with_late, items)
    gathered = (
        result.reshape(blocks_here, GROUP, BS, HD)
        .transpose(0, 2, 1, 3)
        .reshape(span, 1, GROUP * HD)
    )
    returned = lax.all_to_all(
        as_sent(gathered), "uly", split_axis=0, concat_axis=1, tiled=True
    ).astype(gathered.dtype)
    return returned.reshape(tok, kv_heads * GROUP * HD)


def local(queries, keys, values, chosen):
    count = lax.axis_size(AXES)
    if queries.shape[0] == BS and BS % (16 * count) == 0:
        return resident(queries, keys, values, chosen)
    return split_heads(queries, keys, values, chosen)


def solution(mesh):
    placed = (P(AXES, None), P(AXES, None), P(AXES, None), P())
    return jax.shard_map(
        local, mesh=mesh, in_specs=placed, out_specs=P(AXES, None), check_vma=False
    )
```

```python
import functools
import math

import jax
import jax.numpy as jnp
from jax import lax
from jax.experimental import pallas as pl
from jax.experimental.pallas import tpu as pltpu
from jax.sharding import PartitionSpec as P

BS = 512
HD = 128
GROUP = 8
AXES = ("blk", "uly")
TILE = 256
CHUNK = 256
EARLY = 4
CUT = 10
STEP = GROUP
ROOM = 2.0**100
EXPONENT = HD ** (-0.5) * math.log2(math.e)


def scores_of(key_rows, rows):
    return lax.dot_general(
        key_rows, rows, (((1,), (1,)), ((), ())), preferred_element_type=jnp.float32
    )


def weighted(values, scores, top):
    weights = jnp.exp2(scores * EXPONENT - top).astype(jnp.bfloat16)
    both = jnp.dot(values, weights, preferred_element_type=jnp.float32)
    return both[:HD], both[HD : HD + 1]


def over_ones(values, ones):
    return jnp.concatenate([values.T, ones], axis=0)


def staggered(items, first, second):
    held = first(items[0])
    for item, following in zip(items, items[1:] + [None]):
        ahead = first(following) if following else None
        second(item, held)
        held = ahead


def own_kernel(q_ref, k_ref, v_ref, sum_ref, stat_ref):
    keys = k_ref[...]
    values = over_ones(v_ref[...], jnp.ones((16, BS), jnp.bfloat16))
    shape = (TILE, TILE)
    causal = lax.broadcasted_iota(jnp.int32, shape, 0) <= lax.broadcasted_iota(jnp.int32, shape, 1)

    def first(item):
        h, start = item
        rows = q_ref[start : start + TILE, h * HD : (h + 1) * HD]
        return scores_of(keys[: start + TILE], rows)

    def second(item, scores):
        h, start = item
        here = slice(start, start + TILE)
        diagonal = jnp.where(causal, scores[start:], -jnp.inf)
        scores = jnp.concatenate([scores[:start], diagonal], axis=0) if start else diagonal
        top = jnp.max(scores, axis=0, keepdims=True) * EXPONENT
        summed, total = weighted(values[:, : start + TILE], scores, top)
        sum_ref[h * HD : (h + 1) * HD, here] = summed
        stat_ref[h : h + 1, here] = top
        stat_ref[STEP + h : STEP + h + 1, here] = total

    staggered([(h, t) for h in range(STEP) for t in range(0, BS, TILE)], first, second)


def attend_own(queries, keys, values):
    heads = queries.shape[1] // HD
    return pl.pallas_call(
        own_kernel,
        grid=(heads // STEP,),
        in_specs=[
            pl.BlockSpec((BS, STEP * HD), lambda i: (0, i)),
            pl.BlockSpec((BS, HD), lambda i: (0, i * STEP // GROUP)),
            pl.BlockSpec((BS, HD), lambda i: (0, i * STEP // GROUP)),
        ],
        out_specs=[
            pl.BlockSpec((STEP * HD, BS), lambda i: (i, 0)),
            pl.BlockSpec((2 * STEP, BS), lambda i: (i, 0)),
        ],
        out_shape=[
            jax.ShapeDtypeStruct((heads * HD, BS), jnp.float32),
            jax.ShapeDtypeStruct((heads * 2, BS), jnp.float32),
        ],
        compiler_params=pltpu.CompilerParams(vmem_limit_bytes=48 * 2**20),
        cost_estimate=pl.CostEstimate(
            flops=3 * BS * BS * HD * heads,
            bytes_accessed=6 * queries.size,
            transcendentals=BS * BS * heads,
        ),
        name="attend_own",
    )(queries, keys, values)


def routed_kernel(
    usable, q_ref, first_key_ref, sum_hbm, stat_ref, routed_ref, out_hbm, *scratch
):
    sum_ref, part_ref, total_ref, out_ref, sum_sem, out_sems = scratch
    bring = pltpu.make_async_copy(sum_hbm, sum_ref, sum_sem)
    bring.start()
    kv_heads = first_key_ref.shape[1] // HD
    heads = kv_heads * GROUP
    none = jnp.zeros((), jnp.bfloat16)
    ones = jnp.ones((16, BS), jnp.bfloat16)
    keys, values = {}, {}
    for g in range(kv_heads):
        for s in range(2):
            use = usable[g, s] != 0
            some, first_key = routed_ref[:, 2 * g + s], first_key_ref[0:1, g * HD : (g + 1) * HD]
            keys[g, s] = jnp.where(use, some[:, :, :HD].reshape(BS, HD), first_key)
            values[g, s] = over_ones(
                jnp.where(use, some[:, :, HD:].reshape(BS, HD), none), jnp.where(use, ones, none)
            )
    chunks = [(s, c) for s in range(2) for c in range(0, BS, CHUNK)]
    seen = []

    def columns(head, count):
        return pl.ds(head * HD, count * HD)

    def take_out(n, head, count):
        part = columns(head, count)
        return pltpu.make_async_copy(out_ref.at[:, part], out_hbm.at[:, part], out_sems.at[n])

    def stat_rows(h):
        own = h // GROUP * 2 * GROUP + h % GROUP
        return pl.ds(own, 1), pl.ds(GROUP + own, 1)

    def first(item):
        h, start = item
        rows = q_ref[start : start + TILE, h * HD : (h + 1) * HD]
        return [scores_of(keys[h // GROUP, s][c : c + CHUNK], rows) for s, c in chunks]

    def finish(item, summed, total):
        h, start = item
        rows, part = slice(start, start + TILE), columns(h, 1)
        summed = (summed + sum_ref[part, rows]) / total
        out_ref[rows, part] = summed.astype(out_ref.dtype).T

    def second(item, scores):
        h, start = item
        rows = slice(start, start + TILE)
        own_top, own_total = stat_rows(h)
        summed, total = 0.0, stat_ref[own_total, rows]
        for (s, c), some in zip(chunks, scores):
            more = weighted(values[h // GROUP, s][:, c : c + CHUNK], some, stat_ref[own_top, rows])
            summed, total = summed + more[0], total + more[1]
        seen.append(total)
        if h >= EARLY:
            finish(item, summed, total)
            if h == CUT - 1 and start == BS - TILE:
                take_out(0, 0, CUT).start()
            return
        part_ref[columns(h, 1), rows] = summed
        total_ref[h : h + 1, rows] = total
        if h == EARLY - 1 and start == BS - TILE:
            bring.wait()
            for h in range(EARLY):
                for start in range(0, BS, TILE):
                    rows = slice(start, start + TILE)
                    finish((h, start), part_ref[columns(h, 1), rows], total_ref[h : h + 1, rows])

    staggered([(h, t) for h in range(heads) for t in range(0, BS, TILE)], first, second)
    take_out(1, CUT, heads - CUT).start()
    take_out(0, 0, CUT).wait()
    take_out(1, CUT, heads - CUT).wait()
    in_range = functools.reduce(jnp.logical_and, [total < ROOM for total in seen])

    @pl.when(jnp.logical_not(jnp.all(in_range)))
    def _():
        for g in range(kv_heads):
            all_keys = jnp.concatenate([keys[g, s] for s in range(2)], axis=0)
            all_values = jnp.concatenate([values[g, s] for s in range(2)], axis=1)

            @pl.loop(g * GROUP, (g + 1) * GROUP)
            def _(h):
                part = pl.ds(pl.multiple_of(h * HD, HD), HD)
                for start in range(0, BS, TILE):
                    rows = slice(start, start + TILE)
                    own_top, own_total = [stat_ref[at, rows] for at in stat_rows(h)]
                    scores = scores_of(all_keys, q_ref[rows, part])
                    top = jnp.max(scores, axis=0, keepdims=True) * EXPONENT
                    top = jnp.maximum(top, own_top)
                    scale = jnp.exp2(own_top - top)
                    summed, total = weighted(all_values, scores, top)
                    summed = summed + sum_ref[part, rows] * scale
                    total = total + own_total * scale
                    out_ref[rows, part] = (summed / total).astype(out_ref.dtype).T

        again = take_out(0, 0, heads)
        again.start()
        again.wait()


def attend_routed(usable, queries, keys, own_sum, own_stat, routed):
    heads = queries.shape[1] // HD
    vmem, hbm = pl.BlockSpec(memory_space=pltpu.VMEM), pl.BlockSpec(memory_space=pltpu.HBM)
    return pl.pallas_call(
        routed_kernel,
        in_specs=[pl.BlockSpec(memory_space=pltpu.SMEM), vmem, vmem, hbm, vmem, vmem],
        out_specs=hbm,
        out_shape=jax.ShapeDtypeStruct(queries.shape, queries.dtype),
        scratch_shapes=[
            pltpu.VMEM(own_sum.shape, own_sum.dtype),
            pltpu.VMEM((EARLY * HD, BS), jnp.float32),
            pltpu.VMEM((8, BS), jnp.float32),
            pltpu.VMEM(queries.shape, queries.dtype),
            pltpu.SemaphoreType.DMA,
            pltpu.SemaphoreType.DMA((2,)),
        ],
        compiler_params=pltpu.CompilerParams(vmem_limit_bytes=32 * 2**20),
        cost_estimate=pl.CostEstimate(
            flops=8 * BS * BS * HD * heads,
            bytes_accessed=8 * BS * heads * HD + 2 * routed.size,
            transcendentals=2 * BS * BS * heads,
        ),
        name="attend_routed",
    )(usable, queries, keys, pltpu.with_memory_space_constraint(own_sum, pltpu.HBM), own_stat, routed)


def pack_kernel(k_ref, v_ref, out_ref):
    shares, heads, rows, _ = out_ref.shape
    for h in range(heads):
        part = slice(h * HD, (h + 1) * HD)
        out_ref[:, h, :, :HD] = k_ref[:, part].reshape(shares, rows, HD)
        out_ref[:, h, :, HD:] = v_ref[:, part].reshape(shares, rows, HD)


def pack(keys, values, shares):
    shape = (shares, keys.shape[1] // HD, BS // shares, 2 * HD)
    return pl.pallas_call(
        pack_kernel, out_shape=jax.ShapeDtypeStruct(shape, keys.dtype), name="pack"
    )(keys, values)


def resident(queries, keys, values, chosen):
    count = lax.axis_size(AXES)
    me = lax.axis_index(AXES)
    kv_heads = keys.shape[1] // HD
    turn = count // 2
    order = [(p + turn) % count for p in range(count)]
    usable = (lax.dynamic_index_in_dim(chosen, me, 0, keepdims=False) < me).astype(jnp.int32)
    place = (jnp.roll(chosen, -turn, axis=0) + (count - turn)) % count
    wanted = place * kv_heads + jnp.arange(kv_heads, dtype=jnp.int32)[None, :, None]

    def exchange(rows):
        return lax.all_to_all(rows, AXES, 0, 0, axis_index_groups=[order], tiled=True)

    table = exchange(pack(keys, values, count))
    table = table.reshape(count * kv_heads, BS // count, 2 * HD)
    own_sum, own_stat = attend_own(queries, keys, values)
    wanted, own_stat = lax.optimization_barrier((wanted.reshape(-1), own_stat))
    request = table[wanted].reshape(count, kv_heads * 2, BS // count, 2 * HD)
    routed = exchange(request)
    return attend_routed(usable, queries, keys, own_sum, own_stat, routed)


def as_sent(x):
    return jax.tree.map(lambda a: a.astype(jnp.bfloat16) if a.dtype == jnp.float32 else a, x)


def split_heads(queries, keys, values, chosen):
    scale = HD ** (-0.5)
    blk_count = lax.axis_size("blk")
    rank = lax.axis_index("blk")
    head = lax.axis_index("uly")
    tok = queries.shape[0]
    kv_heads = keys.shape[1] // HD
    q_split = queries.reshape(tok, kv_heads, GROUP * HD)
    kv_split = jnp.concatenate(
        [keys.reshape(tok, kv_heads, HD), values.reshape(tok, kv_heads, HD)], axis=2
    )
    q_head, kv_head = (
        lax.all_to_all(q_split, "uly", split_axis=1, concat_axis=0, tiled=True),
        lax.all_to_all(kv_split, "uly", split_axis=1, concat_axis=0, tiled=True),
    )
    span = q_head.shape[0]
    blocks_here = span // BS
    pieces = BS // blk_count
    spread = lax.all_to_all(
        kv_head.reshape(1, blocks_here, blk_count, pieces, 2 * HD),
        "blk",
        split_axis=2,
        concat_axis=0,
        tiled=True,
    )
    table = spread.reshape(blk_count * blocks_here, pieces, 2 * HD)
    wanted = lax.dynamic_index_in_dim(chosen, head, 1, keepdims=False)
    own_ids = lax.dynamic_slice_in_dim(wanted, rank * blocks_here, blocks_here, 0)
    block_ids = rank * blocks_here + jnp.arange(blocks_here, dtype=jnp.int32)
    usable = own_ids < block_ids[:, None]
    q_blocks = q_head.reshape(blocks_here, BS, GROUP, HD)
    own_rows = kv_head.reshape(blocks_here, BS, 2 * HD)
    causal = jnp.arange(BS, dtype=jnp.int32)[None, :] <= jnp.arange(BS, dtype=jnp.int32)[:, None]
    items = jnp.arange(blocks_here * GROUP, dtype=jnp.int32)
    contract = (((1,), (1,)), ((), ()))

    def query_of(item):
        block_q = lax.dynamic_index_in_dim(q_blocks, item // GROUP, 0, keepdims=False)
        return lax.dynamic_index_in_dim(block_q, item % GROUP, 1, keepdims=False)

    def own_part(item):
        query_rows = query_of(item)
        kv_rows = lax.dynamic_index_in_dim(own_rows, item // GROUP, 0, keepdims=False)
        scores = (
            lax.dot_general(
                query_rows, kv_rows[:, :HD], contract, preferred_element_type=jnp.float32
            )
            * scale
        )
        return jnp.where(causal, scores, -jnp.inf)

    def finish(item, own_scores, picked):
        index = item // GROUP
        query_rows = query_of(item)
        own_kv = lax.dynamic_index_in_dim(own_rows, index, 0, keepdims=False)
        routed_kv = lax.dynamic_index_in_dim(picked, index, 0, keepdims=False)
        allowed = lax.dynamic_index_in_dim(usable, index, 0, keepdims=False)
        routed_scores = (
            lax.dot_general(
                query_rows, routed_kv[:, :HD], contract, preferred_element_type=jnp.float32
            )
            * scale
        )
        routed_mask = jnp.repeat(allowed, BS, total_repeat_length=2 * BS)[None, :]
        routed_scores = jnp.where(routed_mask, routed_scores, -jnp.inf)
        top = jnp.maximum(jnp.max(own_scores, axis=-1), jnp.max(routed_scores, axis=-1))[:, None]
        own_weights = jnp.exp(own_scores - top)
        routed_weights = jnp.exp(routed_scores - top)
        total = jnp.sum(own_weights, axis=-1) + jnp.sum(routed_weights, axis=-1)
        summed = jnp.dot(
            own_weights.astype(jnp.bfloat16), own_kv[:, HD:], preferred_element_type=jnp.float32
        )
        summed = summed + jnp.dot(
            routed_weights.astype(jnp.bfloat16),
            routed_kv[:, HD:],
            preferred_element_type=jnp.float32,
        )
        return (summed / total[:, None]).astype(jnp.bfloat16)

    request = table[wanted.reshape(-1)].reshape(blk_count, blocks_here * 2, 1, pieces, 2 * HD)
    arrived = lax.all_to_all(request, "blk", split_axis=0, concat_axis=2, tiled=True)
    picked = arrived.reshape(blocks_here, 2 * BS, 2 * HD)

    def with_late(item):
        return finish(item, own_part(item), picked)

    result = lax.map(with_late, items)
    gathered = (
        result.reshape(blocks_here, GROUP, BS, HD)
        .transpose(0, 2, 1, 3)
        .reshape(span, 1, GROUP * HD)
    )
    returned = lax.all_to_all(
        as_sent(gathered), "uly", split_axis=0, concat_axis=1, tiled=True
    ).astype(gathered.dtype)
    return returned.reshape(tok, kv_heads * GROUP * HD)


def local(queries, keys, values, chosen):
    count = lax.axis_size(AXES)
    if queries.shape[0] == BS and BS % (16 * count) == 0:
        return resident(queries, keys, values, chosen)
    return split_heads(queries, keys, values, chosen)


def solution(mesh):
    placed = (P(AXES, None), P(AXES, None), P(AXES, None), P())
    return jax.shard_map(
        local, mesh=mesh, in_specs=placed, out_specs=P(AXES, None), check_vma=False
    )
```

```python
import functools
import math

import jax
import jax.numpy as jnp
from jax import lax
from jax.experimental import pallas as pl
from jax.experimental.pallas import tpu as pltpu
from jax.sharding import PartitionSpec as P

BS = 512
HD = 128
GROUP = 8
AXES = ("blk", "uly")
TILE = 256
CHUNK = 256
EARLY = 4
CUT = 12
STEP = GROUP
ROOM = 2.0**100
EXPONENT = HD ** (-0.5) * math.log2(math.e)


def scores_of(key_rows, rows):
    return lax.dot_general(
        key_rows, rows, (((1,), (1,)), ((), ())), preferred_element_type=jnp.float32
    )


def weighted(values, scores, top):
    weights = jnp.exp2(scores * EXPONENT - top).astype(jnp.bfloat16)
    both = jnp.dot(values, weights, preferred_element_type=jnp.float32)
    return both[:HD], both[HD : HD + 1]


def over_ones(values, ones):
    return jnp.concatenate([values.T, ones], axis=0)


def staggered(items, first, second):
    held = first(items[0])
    for item, following in zip(items, items[1:] + [None]):
        ahead = first(following) if following else None
        second(item, held)
        held = ahead


def own_kernel(q_ref, k_ref, v_ref, sum_ref, stat_ref):
    keys = k_ref[...]
    values = over_ones(v_ref[...], jnp.ones((16, BS), jnp.bfloat16))
    shape = (TILE, TILE)
    causal = lax.broadcasted_iota(jnp.int32, shape, 0) <= lax.broadcasted_iota(jnp.int32, shape, 1)

    def first(item):
        h, start = item
        rows = q_ref[start : start + TILE, h * HD : (h + 1) * HD]
        return scores_of(keys[: start + TILE], rows)

    def second(item, scores):
        h, start = item
        here = slice(start, start + TILE)
        diagonal = jnp.where(causal, scores[start:], -jnp.inf)
        scores = jnp.concatenate([scores[:start], diagonal], axis=0) if start else diagonal
        top = jnp.max(scores, axis=0, keepdims=True) * EXPONENT
        summed, total = weighted(values[:, : start + TILE], scores, top)
        sum_ref[h * HD : (h + 1) * HD, here] = summed
        stat_ref[h : h + 1, here] = top
        stat_ref[STEP + h : STEP + h + 1, here] = total

    staggered([(h, t) for h in range(STEP) for t in range(0, BS, TILE)], first, second)


def attend_own(queries, keys, values):
    heads = queries.shape[1] // HD
    return pl.pallas_call(
        own_kernel,
        grid=(heads // STEP,),
        in_specs=[
            pl.BlockSpec((BS, STEP * HD), lambda i: (0, i)),
            pl.BlockSpec((BS, HD), lambda i: (0, i * STEP // GROUP)),
            pl.BlockSpec((BS, HD), lambda i: (0, i * STEP // GROUP)),
        ],
        out_specs=[
            pl.BlockSpec((STEP * HD, BS), lambda i: (i, 0)),
            pl.BlockSpec((2 * STEP, BS), lambda i: (i, 0)),
        ],
        out_shape=[
            jax.ShapeDtypeStruct((heads * HD, BS), jnp.float32),
            jax.ShapeDtypeStruct((heads * 2, BS), jnp.float32),
        ],
        compiler_params=pltpu.CompilerParams(vmem_limit_bytes=48 * 2**20),
        cost_estimate=pl.CostEstimate(
            flops=3 * BS * BS * HD * heads,
            bytes_accessed=6 * queries.size,
            transcendentals=BS * BS * heads,
        ),
        name="attend_own",
    )(queries, keys, values)


def routed_kernel(
    usable, q_ref, first_key_ref, sum_hbm, stat_ref, routed_ref, out_hbm, *scratch
):
    sum_ref, part_ref, total_ref, out_ref, sum_sem, out_sems = scratch
    bring = pltpu.make_async_copy(sum_hbm, sum_ref, sum_sem)
    bring.start()
    kv_heads = first_key_ref.shape[1] // HD
    heads = kv_heads * GROUP
    none = jnp.zeros((), jnp.bfloat16)
    ones = jnp.ones((16, BS), jnp.bfloat16)
    keys, values = {}, {}
    for g in range(kv_heads):
        for s in range(2):
            use = usable[g, s] != 0
            some, first_key = routed_ref[:, 2 * g + s], first_key_ref[0:1, g * HD : (g + 1) * HD]
            keys[g, s] = jnp.where(use, some[:, :, :HD].reshape(BS, HD), first_key)
            values[g, s] = over_ones(
                jnp.where(use, some[:, :, HD:].reshape(BS, HD), none), jnp.where(use, ones, none)
            )
    chunks = [(s, c) for s in range(2) for c in range(0, BS, CHUNK)]
    seen = []

    def columns(head, count):
        return pl.ds(head * HD, count * HD)

    def take_out(n, head, count):
        part = columns(head, count)
        return pltpu.make_async_copy(out_ref.at[:, part], out_hbm.at[:, part], out_sems.at[n])

    def stat_rows(h):
        own = h // GROUP * 2 * GROUP + h % GROUP
        return pl.ds(own, 1), pl.ds(GROUP + own, 1)

    def first(item):
        h, start = item
        rows = q_ref[start : start + TILE, h * HD : (h + 1) * HD]
        return [scores_of(keys[h // GROUP, s][c : c + CHUNK], rows) for s, c in chunks]

    def finish(item, summed, total):
        h, start = item
        rows, part = slice(start, start + TILE), columns(h, 1)
        summed = (summed + sum_ref[part, rows]) / total
        out_ref[rows, part] = summed.astype(out_ref.dtype).T

    def second(item, scores):
        h, start = item
        rows = slice(start, start + TILE)
        own_top, own_total = stat_rows(h)
        summed, total = 0.0, stat_ref[own_total, rows]
        for (s, c), some in zip(chunks, scores):
            more = weighted(values[h // GROUP, s][:, c : c + CHUNK], some, stat_ref[own_top, rows])
            summed, total = summed + more[0], total + more[1]
        seen.append(total)
        if h >= EARLY:
            finish(item, summed, total)
            if h == CUT - 1 and start == BS - TILE:
                take_out(0, 0, CUT).start()
            return
        part_ref[columns(h, 1), rows] = summed
        total_ref[h : h + 1, rows] = total
        if h == EARLY - 1 and start == BS - TILE:
            bring.wait()
            for h in range(EARLY):
                for start in range(0, BS, TILE):
                    rows = slice(start, start + TILE)
                    finish((h, start), part_ref[columns(h, 1), rows], total_ref[h : h + 1, rows])

    staggered([(h, t) for h in range(heads) for t in range(0, BS, TILE)], first, second)
    take_out(1, CUT, heads - CUT).start()
    in_range = functools.reduce(jnp.logical_and, [total < ROOM for total in seen])
    redo = jnp.logical_not(jnp.all(in_range))
    take_out(0, 0, CUT).wait()
    take_out(1, CUT, heads - CUT).wait()

    @pl.when(redo)
    def _():
        for g in range(kv_heads):
            all_keys = jnp.concatenate([keys[g, s] for s in range(2)], axis=0)
            all_values = jnp.concatenate([values[g, s] for s in range(2)], axis=1)

            @pl.loop(g * GROUP, (g + 1) * GROUP)
            def _(h):
                part = pl.ds(pl.multiple_of(h * HD, HD), HD)
                for start in range(0, BS, TILE):
                    rows = slice(start, start + TILE)
                    own_top, own_total = [stat_ref[at, rows] for at in stat_rows(h)]
                    scores = scores_of(all_keys, q_ref[rows, part])
                    top = jnp.max(scores, axis=0, keepdims=True) * EXPONENT
                    top = jnp.maximum(top, own_top)
                    scale = jnp.exp2(own_top - top)
                    summed, total = weighted(all_values, scores, top)
                    summed = summed + sum_ref[part, rows] * scale
                    total = total + own_total * scale
                    out_ref[rows, part] = (summed / total).astype(out_ref.dtype).T

        again = take_out(0, 0, heads)
        again.start()
        again.wait()


def attend_routed(usable, queries, keys, own_sum, own_stat, routed):
    heads = queries.shape[1] // HD
    vmem, hbm = pl.BlockSpec(memory_space=pltpu.VMEM), pl.BlockSpec(memory_space=pltpu.HBM)
    return pl.pallas_call(
        routed_kernel,
        in_specs=[pl.BlockSpec(memory_space=pltpu.SMEM), vmem, vmem, hbm, vmem, vmem],
        out_specs=hbm,
        out_shape=jax.ShapeDtypeStruct(queries.shape, queries.dtype),
        scratch_shapes=[
            pltpu.VMEM(own_sum.shape, own_sum.dtype),
            pltpu.VMEM((EARLY * HD, BS), jnp.float32),
            pltpu.VMEM((8, BS), jnp.float32),
            pltpu.VMEM(queries.shape, queries.dtype),
            pltpu.SemaphoreType.DMA,
            pltpu.SemaphoreType.DMA((2,)),
        ],
        compiler_params=pltpu.CompilerParams(vmem_limit_bytes=32 * 2**20),
        cost_estimate=pl.CostEstimate(
            flops=8 * BS * BS * HD * heads,
            bytes_accessed=8 * BS * heads * HD + 2 * routed.size,
            transcendentals=2 * BS * BS * heads,
        ),
        name="attend_routed",
    )(usable, queries, keys, pltpu.with_memory_space_constraint(own_sum, pltpu.HBM), own_stat, routed)


def pack_kernel(k_ref, v_ref, out_ref):
    shares, heads, rows, _ = out_ref.shape
    for h in range(heads):
        part = slice(h * HD, (h + 1) * HD)
        out_ref[:, h, :, :HD] = k_ref[:, part].reshape(shares, rows, HD)
        out_ref[:, h, :, HD:] = v_ref[:, part].reshape(shares, rows, HD)


def pack(keys, values, shares):
    shape = (shares, keys.shape[1] // HD, BS // shares, 2 * HD)
    return pl.pallas_call(
        pack_kernel, out_shape=jax.ShapeDtypeStruct(shape, keys.dtype), name="pack"
    )(keys, values)


def resident(queries, keys, values, chosen):
    count = lax.axis_size(AXES)
    me = lax.axis_index(AXES)
    kv_heads = keys.shape[1] // HD
    usable = (lax.dynamic_index_in_dim(chosen, me, 0, keepdims=False) < me).astype(jnp.int32)
    wanted = chosen * kv_heads + jnp.arange(kv_heads, dtype=jnp.int32)[None, :, None]
    table = lax.all_to_all(pack(keys, values, count), AXES, 0, 0, tiled=True)
    table = table.reshape(count * kv_heads, BS // count, 2 * HD)
    own_sum, own_stat = attend_own(queries, keys, values)
    wanted, own_stat = lax.optimization_barrier((wanted.reshape(-1), own_stat))
    request = table[wanted].reshape(count, kv_heads * 2, BS // count, 2 * HD)
    routed = lax.all_to_all(request, AXES, 0, 0, tiled=True)
    return attend_routed(usable, queries, keys, own_sum, own_stat, routed)


def as_sent(x):
    return jax.tree.map(lambda a: a.astype(jnp.bfloat16) if a.dtype == jnp.float32 else a, x)


def split_heads(queries, keys, values, chosen):
    scale = HD ** (-0.5)
    blk_count = lax.axis_size("blk")
    rank = lax.axis_index("blk")
    head = lax.axis_index("uly")
    tok = queries.shape[0]
    kv_heads = keys.shape[1] // HD
    q_split = queries.reshape(tok, kv_heads, GROUP * HD)
    kv_split = jnp.concatenate(
        [keys.reshape(tok, kv_heads, HD), values.reshape(tok, kv_heads, HD)], axis=2
    )
    q_head, kv_head = (
        lax.all_to_all(q_split, "uly", split_axis=1, concat_axis=0, tiled=True),
        lax.all_to_all(kv_split, "uly", split_axis=1, concat_axis=0, tiled=True),
    )
    span = q_head.shape[0]
    blocks_here = span // BS
    pieces = BS // blk_count
    spread = lax.all_to_all(
        kv_head.reshape(1, blocks_here, blk_count, pieces, 2 * HD),
        "blk",
        split_axis=2,
        concat_axis=0,
        tiled=True,
    )
    table = spread.reshape(blk_count * blocks_here, pieces, 2 * HD)
    wanted = lax.dynamic_index_in_dim(chosen, head, 1, keepdims=False)
    own_ids = lax.dynamic_slice_in_dim(wanted, rank * blocks_here, blocks_here, 0)
    block_ids = rank * blocks_here + jnp.arange(blocks_here, dtype=jnp.int32)
    usable = own_ids < block_ids[:, None]
    q_blocks = q_head.reshape(blocks_here, BS, GROUP, HD)
    own_rows = kv_head.reshape(blocks_here, BS, 2 * HD)
    causal = jnp.arange(BS, dtype=jnp.int32)[None, :] <= jnp.arange(BS, dtype=jnp.int32)[:, None]
    items = jnp.arange(blocks_here * GROUP, dtype=jnp.int32)
    contract = (((1,), (1,)), ((), ()))

    def query_of(item):
        block_q = lax.dynamic_index_in_dim(q_blocks, item // GROUP, 0, keepdims=False)
        return lax.dynamic_index_in_dim(block_q, item % GROUP, 1, keepdims=False)

    def own_part(item):
        query_rows = query_of(item)
        kv_rows = lax.dynamic_index_in_dim(own_rows, item // GROUP, 0, keepdims=False)
        scores = (
            lax.dot_general(
                query_rows, kv_rows[:, :HD], contract, preferred_element_type=jnp.float32
            )
            * scale
        )
        return jnp.where(causal, scores, -jnp.inf)

    def finish(item, own_scores, picked):
        index = item // GROUP
        query_rows = query_of(item)
        own_kv = lax.dynamic_index_in_dim(own_rows, index, 0, keepdims=False)
        routed_kv = lax.dynamic_index_in_dim(picked, index, 0, keepdims=False)
        allowed = lax.dynamic_index_in_dim(usable, index, 0, keepdims=False)
        routed_scores = (
            lax.dot_general(
                query_rows, routed_kv[:, :HD], contract, preferred_element_type=jnp.float32
            )
            * scale
        )
        routed_mask = jnp.repeat(allowed, BS, total_repeat_length=2 * BS)[None, :]
        routed_scores = jnp.where(routed_mask, routed_scores, -jnp.inf)
        top = jnp.maximum(jnp.max(own_scores, axis=-1), jnp.max(routed_scores, axis=-1))[:, None]
        own_weights = jnp.exp(own_scores - top)
        routed_weights = jnp.exp(routed_scores - top)
        total = jnp.sum(own_weights, axis=-1) + jnp.sum(routed_weights, axis=-1)
        summed = jnp.dot(
            own_weights.astype(jnp.bfloat16), own_kv[:, HD:], preferred_element_type=jnp.float32
        )
        summed = summed + jnp.dot(
            routed_weights.astype(jnp.bfloat16),
            routed_kv[:, HD:],
            preferred_element_type=jnp.float32,
        )
        return (summed / total[:, None]).astype(jnp.bfloat16)

    request = table[wanted.reshape(-1)].reshape(blk_count, blocks_here * 2, 1, pieces, 2 * HD)
    arrived = lax.all_to_all(request, "blk", split_axis=0, concat_axis=2, tiled=True)
    picked = arrived.reshape(blocks_here, 2 * BS, 2 * HD)

    def with_late(item):
        return finish(item, own_part(item), picked)

    result = lax.map(with_late, items)
    gathered = (
        result.reshape(blocks_here, GROUP, BS, HD)
        .transpose(0, 2, 1, 3)
        .reshape(span, 1, GROUP * HD)
    )
    returned = lax.all_to_all(
        as_sent(gathered), "uly", split_axis=0, concat_axis=1, tiled=True
    ).astype(gathered.dtype)
    return returned.reshape(tok, kv_heads * GROUP * HD)


def local(queries, keys, values, chosen):
    count = lax.axis_size(AXES)
    if queries.shape[0] == BS and BS % (16 * count) == 0:
        return resident(queries, keys, values, chosen)
    return split_heads(queries, keys, values, chosen)


def solution(mesh):
    placed = (P(AXES, None), P(AXES, None), P(AXES, None), P())
    return jax.shard_map(
        local, mesh=mesh, in_specs=placed, out_specs=P(AXES, None), check_vma=False
    )
```
